256 devices in a mesh: row: 8 (over x, core), col: 32 (over z, y).
Axes of the slice: x: 4, y: 4, z: 8, core: 2. Of those that a mesh axis runs over, the one named last changes fastest.
Arguments:
- matrix: bfloat16 [12, 2048, 3, 8192], P(None, 'row', None, 'col'), may hold values from -5 to 101, as said below
Outputs:
- factored: bfloat16 [12, 2048, 3, 8192], P(None, 'row', None, 'col')
The draws below stay inside these ranges and needn't reach their ends.
Inputs may be any that keep to these rules, and one draw needn't show every extreme that they name: `matrix`: each diagonal entry is a value between 4 * sqrt(256) and 6 * sqrt(256) plus an entry of order one; every other entry is of order one.
All inputs are finite; a program needn't handle non-finite values.
Results may differ from the reference program's by a relative error of at most 0.0052.
Values may be sent and summed in bfloat16 or wider, within the bound.
A program may use at most 64 MiB of HBM per device.

```python
import jax
import jax.numpy as jnp
from jax import lax

NB = 256
BC = 3
STEPS = 2
BR = 12
N_ROW = 8
N_COL = 32


def draw_matrix(key, part):
    key = jax.random.fold_in(key, 7)
    key_off, key_diag = jax.random.split(key)
    shape = (BR, N_ROW * NB, BC, N_COL * NB)
    grow = lax.broadcasted_iota(jnp.int32, (BR, N_ROW * NB, 1, 1), 0) * (N_ROW * NB) + lax.broadcasted_iota(jnp.int32, (BR, N_ROW * NB, 1, 1), 1)
    gcol = lax.broadcasted_iota(jnp.int32, (1, 1, BC, N_COL * NB), 2) * (N_COL * NB) + lax.broadcasted_iota(jnp.int32, (1, 1, BC, N_COL * NB), 3)
    root = NB ** 0.5
    off = jnp.clip(jax.random.normal(key_off, shape, jnp.float32), -5.0, 5.0)
    heavy = jax.random.uniform(key_diag, (BR, N_ROW * NB, 1, 1), jnp.float32, 4.5 * root, 5.5 * root)
    return jnp.where(grow == gcol, heavy + off, off).astype(jnp.bfloat16)


def setup_inputs(seed: int = 0) -> dict:
    key_of = jax.random.split(jax.random.key(seed), 2)
    matrix = draw_matrix(jax.random.fold_in(key_of[1], 71), 0)
    return dict(matrix=matrix)


def factor_block(block):
    size = block.shape[0]
    idx = jnp.arange(size)

    def turn(j, work):
        pivot = lax.dynamic_slice(work, (j, j), (1, 1))[0, 0]
        column = lax.dynamic_slice_in_dim(work, j, 1, 1)[:, 0]
        row_vals = lax.dynamic_slice_in_dim(work, j, 1, 0)[0]
        below = idx > j
        lcol = jnp.where(below, column / pivot, jnp.zeros_like(column))
        urow = jnp.where(below, row_vals, jnp.zeros_like(row_vals))
        work = work - lcol[:, None] * urow[None, :]
        return jnp.where(below[:, None] & (idx == j)[None, :], lcol[:, None], work)

    return lax.fori_loop(0, size, turn, block)


def series_inverse(strict):
    size = strict.shape[0]
    eye = jnp.eye(size, dtype=strict.dtype)
    term = -strict
    result = eye + term
    for level in range((size - 1).bit_length() - 1):
        term = jnp.dot(term, term, precision=lax.Precision.HIGHEST)
        result = jnp.dot(result, eye + term, precision=lax.Precision.HIGHEST)
    return result


def invert_factors(packed):
    diag_vals = jnp.diagonal(packed)
    linv = series_inverse(jnp.tril(packed, -1))
    scaled = jnp.triu(packed, 1) / diag_vals[:, None]
    uinv = series_inverse(scaled) / diag_vals[None, :]
    return linv.astype(jnp.bfloat16), uinv.astype(jnp.bfloat16)


def reference(matrix):
    order = matrix.shape[0] * matrix.shape[1]
    nblk = order // NB
    full = matrix.reshape(order, order)
    positions = jnp.arange(order)
    for k in range(STEPS):
        start = k * NB
        end = start + NB
        packed = factor_block(full[start:end, start:end].astype(jnp.float32))
        linv, uinv = invert_factors(packed)
        lower = jnp.dot(full[:, start:end], uinv, preferred_element_type=jnp.float32).astype(jnp.bfloat16)
        lpanel = jnp.where((positions >= end)[:, None], lower, jnp.zeros_like(lower))
        upper = jnp.dot(linv, full[start:end, :], preferred_element_type=jnp.float32).astype(jnp.bfloat16)
        upanel = jnp.where((positions >= end)[None, :], upper, jnp.zeros_like(upper))

        def apply_rows(pair):
            rows_blk, lower_blk = pair
            change = jnp.dot(lower_blk, upanel, preferred_element_type=jnp.float32)
            return (rows_blk.astype(jnp.float32) - change).astype(jnp.bfloat16)

        full = lax.map(apply_rows, (full.reshape(nblk, NB, order), lpanel.reshape(nblk, NB, NB)))
        full = full.reshape(order, order)
        full = full.at[end:, start:end].set(lpanel[end:])
        full = full.at[start:end, start:end].set(packed.astype(jnp.bfloat16))
        full = full.at[start:end, end:].set(upanel[:, end:])
    return full.reshape(matrix.shape)
```

```python
import functools

import jax
import jax.experimental.pallas as pl
import jax.experimental.pallas.tpu as pltpu
import jax.numpy as jnp
from jax import lax
from jax.sharding import PartitionSpec as P

NB = 256
B = 64
BR, BC = 12, 3
N_ROW, N_COL, N_Y, N_Z = 8, 32, 4, 8
F32, BF = jnp.float32, jnp.bfloat16
MESH = pl.DeviceIdType.MESH
CHUNKS = 2 * BR


def recip(p):
    r = pl.reciprocal(p, approx=True)
    return r * (2.0 - p * r)

def bcast_lane(t, n):
    return jnp.broadcast_to(t[:, n:n + 1], (8, 128))

def bcast_row(t, j):
    return jnp.broadcast_to(t[j:j + 1, :], (8, 128))

def base(m1, m2, tick):
    sub = lax.broadcasted_iota(jnp.int32, (8, 128), 0)
    for k in range(8):
        tick(k)
        n = range(k, 8)
        v = {i: [bcast_lane(m1[i], 8 * k + j) for j in range(8)] for i in n}
        w = {i: [bcast_lane(m2[i], 8 * k + j) for j in range(8)] for i in n}
        scale = jnp.ones((8, 128), F32)
        for j in range(8):
            r = recip(bcast_row(v[k][j], j))
            scale = jnp.where(sub == j, r, scale)
            lv = {i: v[i][j] * r for i in n}
            lw = {i: w[i][j] * r for i in n}
            lv[k] = jnp.where(sub > j, lv[k], 0.0)
            lw[k] = jnp.where(sub > j, lw[k], 0.0)
            for t in range(j + 1, 8):
                a, b = bcast_row(v[k][t], j), bcast_row(w[k][t], j)
                for i in n:
                    v[i][t] = v[i][t] - lv[i] * a
                    w[i][t] = w[i][t] - lw[i] * b
            a, b = bcast_row(m1[k], j), bcast_row(m2[k], j)
            for i in n:
                m1[i] = m1[i] - lv[i] * a
                m2[i] = m2[i] - lw[i] * b
        m2[k] = m2[k] * scale
    return jnp.concatenate(m1, 0), jnp.concatenate(m2, 0)

def split(a):
    h = a.astype(BF)
    return h, (a - h.astype(F32)).astype(BF)

def dot3(a, b, nt=False):
    d = functools.partial(lax.dot_general, dimension_numbers=(((1,), (1 if nt else 0,)), ((), ())), preferred_element_type=F32)
    return d(a[0], b[0]) + (d(a[0], b[1]) + d(a[1], b[0]))

def block_step(q, a1, a2, tick):
    rows = pl.ds(pl.multiple_of(q * B, B), B)
    odd = lax.rem(q, 2) == 1
    half = lax.div(q, 2)
    lane = lax.broadcasted_iota(jnp.int32, (B, 128), 1)
    sub = lax.broadcasted_iota(jnp.int32, (B, 128), 0)
    eye = (lane - B == sub).astype(F32)
    def diag(a):
        x = a[half, rows, :]
        x = jnp.where(odd, pltpu.roll(x, B, 1), x)
        x = jnp.where(lane < B, x, eye)
        return [x[8 * i:8 * i + 8] for i in range(8)]
    m1, m2 = base(diag(a1), diag(a2), tick)
    r1, r2 = pltpu.roll(m1, B, 1), pltpu.roll(m2, B, 1)
    mine = (lane >= B) == odd
    li, ui = r1[:, :B], r2[:, :B]
    lip = split(jnp.where(mine, jnp.where(odd, m1, r1), 0.0))
    uip = split(jnp.where(mine, jnp.where(odd, m2, r2), 0.0))
    below = lax.broadcasted_iota(jnp.int32, (256, B), 0) >= (q + 1) * B
    l21 = split(jnp.where(below, dot3(split(a1[half]), uip, True), 0.0))
    u12 = split(jnp.where(below, dot3(split(a2[half]), lip, True), 0.0))
    for a, li_, mult, m, r in ((a1, split(li), l21, m1, r1), (a2, split(ui), u12, m2, r2)):
        old = a[:, rows, :]
        p = dot3(li_, split(jnp.concatenate([old[i] for i in range(4)], 1)))
        prod = dot3(mult, split(p))
        for i in range(4):
            a[i] = a[i] - prod[:, 128 * i:128 * i + 128]
            a[i, rows, :] = p[:, 128 * i:128 * i + 128]
        a[half, rows, :] = jnp.where(mine, jnp.where(odd, r, m), a[half, rows, :])

def load(a, a1, a2):
    eye = (lax.broadcasted_iota(jnp.int32, (256, 256), 0) == lax.broadcasted_iota(jnp.int32, (256, 256), 1)).astype(F32)
    for ref, x in ((a1, a), (a2, jnp.transpose(a))):
        for i in range(2):
            ref[i] = x[:, 128 * i:128 * i + 128]
            ref[2 + i] = eye[:, 128 * i:128 * i + 128]

def full(a, i):
    return jnp.concatenate([a[i], a[i + 1]], 1)

def results(a1, a2):
    ri = lax.broadcasted_iota(jnp.int32, (256, 256), 0); ci = lax.broadcasted_iota(jnp.int32, (256, 256), 1)
    packed = jnp.where(ri <= ci, full(a1, 0), jnp.transpose(full(a2, 0)))
    return packed, full(a1, 2), jnp.transpose(full(a2, 2))


def nn(a, b):
    return jnp.dot(a, b, preferred_element_type=F32)


def gather_factor(
    a, col_out, row_out, packed, linv, uinv, l10_out, u01_out,
    col, row, pieces, a1, a2,
    s1_send, s2_send, s3_send, p_recv, s3_recv,
    col_send, col_recv, row_send, row_recv, local_sem,
):
    r, c = lax.axis_index("row"), lax.axis_index("col")
    z, y = lax.div(c, N_Y), lax.rem(c, N_Y)
    core = lax.rem(r, 2)

    def send(src, dst, ssem, rsem, dev):
        return pltpu.make_async_remote_copy(
            src_ref=src, dst_ref=dst, send_sem=ssem, recv_sem=rsem, device_id=dev, device_id_type=MESH
        )

    barrier = pltpu.get_barrier_semaphore()

    @pl.loop(1, N_COL)
    def _(i):
        pl.semaphore_signal(barrier, inc=1, device_id=(r, lax.rem(c + i, N_COL)), device_id_type=MESH)

    @pl.loop(1, N_ROW)
    def _(i):
        pl.semaphore_signal(barrier, inc=1, device_id=(lax.rem(r + i, N_ROW), c), device_id_type=MESH)

    pl.semaphore_wait(barrier, N_COL - 1 + N_ROW - 1)

    def diag_piece(p):
        return a.at[0, 0, lax.div(p, 16), pl.ds(pl.multiple_of(lax.rem(lax.div(p, 2), 8) * 16, 16), 16),
                    pl.ds(pl.multiple_of(lax.rem(p, 2) * 128, 128), 128)]

    def own_copy(b):
        return pltpu.make_async_copy(diag_piece(c), pieces.at[b, c], p_recv.at[b])

    for b in range(4):
        @pl.when((r == b // 2) & (c == b % 2))
        def _(b=b):
            @pl.loop(1, N_COL)
            def _(i):
                dst = lax.rem(c + i, N_COL)
                send(diag_piece(dst), pieces.at[b, dst], s1_send.at[0], p_recv.at[b], (r, dst)).start()

            own_copy(b).start()

    dist_z = jnp.minimum(z, N_Z - z)
    dist_y = [lax.rem(y - b + N_Y, N_Y) for b in range(2)]
    source = [(z == 0) & (dist_y[b] == 0) for b in range(2)]

    def load_panel(b):
        return pltpu.make_async_copy(a.at[:, 0], col.at[b], local_sem.at[0])

    def load_row():
        return pltpu.make_async_copy(a.at[0], row.at[core], local_sem.at[1])

    for b in range(2):
        @pl.when(source[b])
        def _(b=b):
            load_panel(b).start()

    @pl.when(r < 2)
    def _():
        load_row().start()

    def arrived(b):
        own = (r == b // 2) & (c == b % 2)

        @pl.when(own)
        def _():
            own_copy(b).wait()

        @pl.when(jnp.logical_not(own))
        def _():
            send(pieces.at[b, c], pieces.at[b, c], s1_send.at[0], p_recv.at[b], (r, c)).wait_recv()

    def to_rows(b):
        for i in range(1, N_ROW):
            dst = lax.rem(r + i, N_ROW)
            yield send(pieces.at[b, c], pieces.at[b, c], s2_send.at[b % 2, i - 1], p_recv.at[b], (dst, c))

    def spread_rows(blocks):
        for b in blocks:
            @pl.when(r == b // 2)
            def _(b=b):
                arrived(b)
                for copy in to_rows(b):
                    copy.start()

    def to_cols(kind, dst):
        block = pieces.at[pl.ds(kind, 1 + 2 * kind), c]
        return send(block, block, s3_send.at[kind], s3_recv.at[kind], (r, dst))

    def spread_cols(kind, blocks):
        for b in blocks:
            @pl.when(r != b // 2)
            def _(b=b):
                arrived(b)

        @pl.loop(1, N_COL)
        def _(i):
            to_cols(kind, lax.rem(c + i, N_COL)).start()

    def all_pieces(kind):
        block = pieces.at[pl.ds(kind, 1 + 2 * kind), pl.ds(0, N_COL - 1)]
        return send(block, block, s3_send.at[kind], s3_recv.at[kind], (r, c))

    spread_rows((0,))
    spread_cols(0, (0,))
    for b in range(2):
        @pl.when(source[b])
        def _(b=b):
            load_panel(b).wait()

    @pl.when(r < 2)
    def _():
        load_row().wait()

    def forwards(b, half):
        z_up = (dist_y[b] == 0) & (z <= 3)
        z_down = (dist_y[b] == 0) & ((z == 0) | (z >= 6))
        if half == 0:
            y_on, y_dst = dist_y[b] <= 2, lax.rem(y + 1, N_Y)
        else:
            y_on, y_dst = dist_y[b] != 1, lax.rem(y + N_Y - 1, N_Y)
        z_dst = lambda dz: lax.rem(z + dz + N_Z, N_Z) * N_Y + y
        return ((z_up, z_dst(1)), (z_down, z_dst(-1)), (y_on, z * N_Y + y_dst))

    def chunk_copy(b, half, i, way, dst):
        block = col.at[b, i, half]
        return send(block, block, col_send.at[b, half, i, way], col_recv.at[b, half, i], (r, dst))

    def relay(slot):
        for b in range(2):
            for half in range(2):
                dist = dist_z + (dist_y[b] if half == 0 else lax.rem(N_Y - dist_y[b], N_Y))
                m = slot - dist - (2 * half + b)
                i = lax.div(m, 4)

                @pl.when((m >= 0) & (lax.rem(m, 4) == 0) & (i < BR))
                def _(b=b, half=half, i=i):
                    @pl.when(jnp.logical_not(source[b]))
                    def _():
                        chunk_copy(b, half, i, 0, c).wait_recv()

                    for way, (on, dst) in enumerate(forwards(b, half)):
                        @pl.when(on)
                        def _(way=way, dst=dst):
                            chunk_copy(b, half, i, way, dst).start()

    def row_copy(i, dst):
        block = row.at[core]
        return send(block, block, row_send.at[i], row_recv.at[core], (dst, c))

    def row_out_start():
        @pl.when(r < 2)
        def _():
            for i in range(1, 4):
                row_copy(i, r + 2 * i).start()

    def row_swap():
        @pl.when(r >= 2)
        def _():
            row_copy(0, r).wait_recv()

        row_copy(0, r + 1 - 2 * core).start()

    send(pieces.at[0, pl.ds(0, N_COL - 1)], pieces.at[0, pl.ds(0, N_COL - 1)],
         s3_send.at[0], s3_recv.at[0], (r, c)).wait_recv()

    def whole(b):
        x = pieces[b].astype(F32).reshape(16, 2, 16, 128)
        return jnp.concatenate([x[:, 0].reshape(NB, 128), x[:, 1].reshape(NB, 128)], 1)

    load(whole(0), a1, a2)

    @pl.loop(0, 8)
    def _(it):
        step = lax.div(it, 4)
        q = lax.rem(it, 4)

        @pl.when(it == 4)
        def _():
            all_pieces(1).wait_recv()
            l10 = nn(whole(2).astype(BF), uinv[0]).astype(BF)
            u01 = nn(linv[0], whole(1).astype(BF)).astype(BF)
            l10_out[...] = l10
            u01_out[...] = u01
            load((whole(3) - nn(l10, u01)).astype(BF).astype(F32), a1, a2)

        def tick(k):
            relay(it * 8 + k)
            if k == 1:
                @pl.when(it == 0)
                def _():
                    spread_rows((1, 2, 3))

            if k == 3:
                @pl.when(it == 0)
                def _():
                    spread_cols(1, (1, 2, 3))

            if k == 5:
                @pl.when(it == 0)
                def _():
                    row_out_start()

                @pl.when(it == 5)
                def _():
                    row_swap()

        block_step(q, a1, a2, tick)

        @pl.when(q == 3)
        def _():
            pk, li, ui = results(a1, a2)
            packed[step] = pk.astype(BF)
            linv[step] = li.astype(BF)
            uinv[step] = ui.astype(BF)

    out_copies = [
        pltpu.make_async_copy(col, col_out, local_sem.at[0]),
        pltpu.make_async_copy(row, row_out, local_sem.at[1]),
    ]
    out_copies[0].start()
    other = row.at[1 - core]
    send(other, other, row_send.at[0], row_recv.at[1 - core], (r, c)).wait_recv()
    out_copies[1].start()

    for b in range(4):
        @pl.when((r == b // 2) & (c == b % 2))
        def _(b=b):
            block = pieces.at[0, pl.ds(0, N_COL - 1)]
            send(block, block, s1_send.at[0], p_recv.at[b], (r, c)).wait_send()

        @pl.when(r == b // 2)
        def _(b=b):
            for copy in to_rows(b):
                copy.wait_send()

    for kind in range(2):
        all_pieces(kind).wait_send()

    @pl.when(r < 2)
    def _():
        for i in range(1, 4):
            row_copy(i, r).wait_send()

    row_copy(0, r).wait_send()

    for b in range(2):
        for half in range(2):
            for way, (on, dst) in enumerate(forwards(b, half)):
                @pl.when(on)
                def _(b=b, half=half, way=way, dst=dst):
                    @pl.loop(0, BR)
                    def _(i):
                        chunk_copy(b, half, i, way, dst).wait_send()

    for copy in out_copies:
        copy.wait()


def update(a, col, row, packed, linv, uinv, l10, u01, out, u):
    i = pl.program_id(0)
    r, c = lax.axis_index("row"), lax.axis_index("col")

    @pl.when(i == 0)
    def _():
        for j in range(BC):
            h = j * N_COL + c
            u0 = jnp.where(h > 0, nn(linv[0], row[0, j]), 0.0).astype(BF)
            r1 = (row[1, j].astype(F32) - nn(l10[...], u0)).astype(BF)
            u[0, j] = u0
            u[1, j] = jnp.where(h > 1, nn(linv[1], r1), 0.0).astype(BF)

    g = i * N_ROW + r
    l0 = jnp.where(g > 0, nn(col[0], uinv[0]), 0.0).astype(BF)
    c1 = (col[1].astype(F32) - nn(l0, u01[...])).astype(BF)
    l1 = jnp.where(g > 1, nn(c1, uinv[1]), 0.0).astype(BF)
    for j in range(BC):
        x = (a[j].astype(F32) - nn(l0, u[0, j])).astype(BF)
        out[j] = (x.astype(F32) - nn(l1, u[1, j])).astype(BF)

    @pl.when(c == 0)
    def _():
        out[0] = jnp.where(g > 0, l0, packed[0])

    @pl.when(c == 1)
    def _():
        out[0] = jnp.where(g > 1, l1, jnp.where(g == 1, packed[1], out[0]))

    @pl.when(i == 0)
    def _():
        for j in range(BC):
            h = j * N_COL + c
            out[j] = jnp.where((r == 0) & (h > 0), u[0, j], jnp.where((r == 1) & (h > 1), u[1, j], out[j]))


def on_device(matrix):
    a = matrix.transpose(0, 2, 1, 3)
    vmem = pl.BlockSpec(memory_space=pltpu.VMEM)
    hbm = pl.BlockSpec(memory_space=pl.ANY)
    shape = jax.ShapeDtypeStruct
    dma = pltpu.SemaphoreType.DMA
    col, row, packed, linv, uinv, l10, u01 = pl.pallas_call(
        gather_factor,
        out_shape=[
            shape((2, BR, 2, 128, NB), BF),
            shape((2, BC, 2, 128, NB), BF),
            shape((2, NB, NB), BF),
            shape((2, NB, NB), BF),
            shape((2, NB, NB), BF),
            shape((NB, NB), BF),
            shape((NB, NB), BF),
        ],
        in_specs=[hbm],
        out_specs=[hbm, hbm] + [vmem] * 5,
        scratch_shapes=[
            pltpu.VMEM((2, BR, 2, 128, NB), BF),
            pltpu.VMEM((2, BC, 2, 128, NB), BF),
            pltpu.VMEM((4, N_COL, 16, 128), BF),
            pltpu.VMEM((4, NB, 128), F32),
            pltpu.VMEM((4, NB, 128), F32),
            dma((1,)), dma((2, N_ROW - 1)), dma((2,)), dma((4,)), dma((2,)),
            dma((2, 2, BR, 3)), dma((2, 2, BR)), dma((4,)), dma((2,)), dma((2,)),
        ],
        compiler_params=pltpu.CompilerParams(
            collective_id=0, has_side_effects=True, vmem_limit_bytes=40 << 20
        ),
        name="gather_factor",
    )(a.reshape(BR, BC, 2, 128, NB))
    whole = lambda *dims: pl.BlockSpec(dims, lambda i: (0,) * len(dims))
    out = pl.pallas_call(
        update,
        grid=(BR,),
        out_shape=shape((BR, BC, NB, NB), BF),
        in_specs=[
            pl.BlockSpec((None, BC, NB, NB), lambda i: (i, 0, 0, 0)),
            pl.BlockSpec((2, None, NB, NB), lambda i: (0, i, 0, 0)),
            whole(2, BC, NB, NB),
            whole(2, NB, NB),
            whole(2, NB, NB),
            whole(2, NB, NB),
            whole(NB, NB),
            whole(NB, NB),
        ],
        out_specs=pl.BlockSpec((None, BC, NB, NB), lambda i: (i, 0, 0, 0)),
        scratch_shapes=[pltpu.VMEM((2, BC, NB, NB), BF)],
        compiler_params=pltpu.CompilerParams(vmem_limit_bytes=40 << 20),
        name="update",
    )(a, col.reshape(2, BR, NB, NB), row.reshape(2, BC, NB, NB), packed, linv, uinv, l10, u01)
    return out.transpose(0, 2, 1, 3)


def solution(mesh):
    placed = (P(None, "row", None, "col"),)
    return jax.shard_map(
        on_device,
        mesh=mesh,
        in_specs=placed,
        out_specs=P(None, "row", None, "col"),
        check_vma=False,
    )
```

```python
import functools

import jax
import jax.experimental.pallas as pl
import jax.experimental.pallas.tpu as pltpu
import jax.numpy as jnp
from jax import lax
from jax.sharding import PartitionSpec as P

NB = 256
B = 64
BR, BC = 12, 3
N_ROW, N_COL, N_Y, N_Z = 8, 32, 4, 8
F32, BF = jnp.float32, jnp.bfloat16
MESH = pl.DeviceIdType.MESH
HOP = 8
PRE1, PRE2 = 4, 16
TAIL = 3
assert all(PRE2 + 64 + TAIL * (i + 1) >= 6 * HOP + 5 * i + 4 for i in range(BR))


def recip(p):
    r = pl.reciprocal(p, approx=True)
    return r * (2.0 - p * r)

def bcast_lane(t, n):
    return jnp.broadcast_to(t[:, n:n + 1], (8, 128))

def bcast_row(t, j):
    return jnp.broadcast_to(t[j:j + 1, :], (8, 128))

def base(m1, m2, tick):
    sub = lax.broadcasted_iota(jnp.int32, (8, 128), 0)
    for k in range(8):
        tick(k)
        n = range(k, 8)
        v = {i: [bcast_lane(m1[i], 8 * k + j) for j in range(8)] for i in n}
        w = {i: [bcast_lane(m2[i], 8 * k + j) for j in range(8)] for i in n}
        scale = jnp.ones((8, 128), F32)
        for j in range(8):
            r = recip(bcast_row(v[k][j], j))
            scale = jnp.where(sub == j, r, scale)
            lv = {i: v[i][j] * r for i in n}
            lw = {i: w[i][j] * r for i in n}
            lv[k] = jnp.where(sub > j, lv[k], 0.0)
            lw[k] = jnp.where(sub > j, lw[k], 0.0)
            for t in range(j + 1, 8):
                a, b = bcast_row(v[k][t], j), bcast_row(w[k][t], j)
                for i in n:
                    v[i][t] = v[i][t] - lv[i] * a
                    w[i][t] = w[i][t] - lw[i] * b
            a, b = bcast_row(m1[k], j), bcast_row(m2[k], j)
            for i in n:
                m1[i] = m1[i] - lv[i] * a
                m2[i] = m2[i] - lw[i] * b
        m2[k] = m2[k] * scale
    return jnp.concatenate(m1, 0), jnp.concatenate(m2, 0)

def split(a):
    h = a.astype(BF)
    return h, (a - h.astype(F32)).astype(BF)

def dot3(a, b, nt=False):
    d = functools.partial(lax.dot_general, dimension_numbers=(((1,), (1 if nt else 0,)), ((), ())), preferred_element_type=F32)
    return d(a[0], b[0]) + (d(a[0], b[1]) + d(a[1], b[0]))

def factor(a1, a2, tick):
    eye = (lax.broadcasted_iota(jnp.int32, (B, B), 0) == lax.broadcasted_iota(jnp.int32, (B, B), 1)).astype(F32)
    for q in range(NB // B):
        s, e = q * B, (q + 1) * B
        d1 = jnp.concatenate([a1[s:e, s:e], eye], axis=1)
        d2 = jnp.concatenate([a2[s:e, s:e], eye], axis=1)
        m1, m2 = base(
            [d1[8 * i : 8 * i + 8] for i in range(8)], [d2[8 * i : 8 * i + 8] for i in range(8)],
            lambda k, q=q: tick(8 * q + k),
        )
        li, ui = split(m1[:, B:]), split(m2[:, B:])
        p1, p2 = dot3(li, split(a1[s:e, :])), dot3(ui, split(a2[s:e, :]))
        if e < NB:
            l21 = split(dot3(split(a1[e:, s:e]), ui, True))
            u12 = split(dot3(split(a2[e:, s:e]), li, True))
            a1[e:, :] = a1[e:, :] - dot3(l21, split(p1))
            a2[e:, :] = a2[e:, :] - dot3(u12, split(p2))
        a1[s:e, :] = p1
        a2[s:e, :] = p2
        a1[s:e, s:e] = m1[:, :B]
        a2[s:e, s:e] = m2[:, :B]


def load(a, a1, a2):
    ri = lax.broadcasted_iota(jnp.int32, (NB, NB), 0)
    ci = lax.broadcasted_iota(jnp.int32, (NB, NB), 1)
    eye = (ri == ci).astype(F32)
    for ref, x in ((a1, a), (a2, jnp.transpose(a))):
        ref[:, :NB] = x
        ref[:, NB:] = eye


def results(a1, a2):
    ri = lax.broadcasted_iota(jnp.int32, (NB, NB), 0)
    ci = lax.broadcasted_iota(jnp.int32, (NB, NB), 1)
    packed = jnp.where(ri <= ci, a1[:, :NB], jnp.transpose(a2[:, :NB]))
    return packed, a1[:, NB:], jnp.transpose(a2[:, NB:])


def nn(a, b):
    return jnp.dot(a, b, preferred_element_type=F32)


def gather_factor(
    a, mine, packed, linv, uinv, l10, u01, u, col, row, pieces, a1, a2,
    s1_send, s2_send, s3_send, p_recv, s3_recv,
    col_send, col_recv, row_send, row_recv, local_sem,
):
    r, c = lax.axis_index("row"), lax.axis_index("col")
    z, y = lax.div(c, N_Y), lax.rem(c, N_Y)
    core = lax.rem(r, 2)

    def send(src, dst, ssem, rsem, dev):
        return pltpu.make_async_remote_copy(
            src_ref=src, dst_ref=dst, send_sem=ssem, recv_sem=rsem, device_id=dev, device_id_type=MESH
        )

    barrier = pltpu.get_barrier_semaphore()

    @pl.loop(1, N_COL)
    def _(i):
        pl.semaphore_signal(barrier, inc=1, device_id=(r, lax.rem(c + i, N_COL)), device_id_type=MESH)

    @pl.loop(1, N_ROW)
    def _(i):
        pl.semaphore_signal(barrier, inc=1, device_id=(lax.rem(r + i, N_ROW), c), device_id_type=MESH)

    pl.semaphore_wait(barrier, N_COL - 1 + N_ROW - 1)

    def diag_piece(p):
        return a.at[0, 0, lax.div(p, 8), pl.ds(pl.multiple_of(lax.rem(lax.div(p, 2), 4) * 16, 16), 16),
                    pl.ds(pl.multiple_of(lax.rem(p, 2) * 128, 128), 128)]

    def own_copy(b):
        return pltpu.make_async_copy(diag_piece(c), pieces.at[b, c], p_recv.at[b])

    for b in range(4):
        @pl.when((r == b // 2) & (c == b % 2))
        def _(b=b):
            @pl.loop(1, N_COL)
            def _(i):
                dst = lax.rem(c + i, N_COL)
                send(diag_piece(dst), pieces.at[b, dst], s1_send.at[0], p_recv.at[b], (r, dst)).start()

            own_copy(b).start()

    dist_z = jnp.where(z == 0, 0, jnp.where(lax.rem(z, 4) == 2, 1, jnp.where(z == 4, 3, 2)))
    dist_y = [lax.rem(y - b + N_Y, N_Y) for b in range(2)]
    source = [(z == 0) & (dist_y[b] == 0) for b in range(2)]

    def load_panel(b):
        return pltpu.make_async_copy(a.at[:, 0], col.at[b], local_sem.at[0])

    def load_row():
        return pltpu.make_async_copy(a.at[0], row.at[core], local_sem.at[1])

    for b in range(2):
        @pl.when(source[b])
        def _(b=b):
            load_panel(b).start()

    @pl.when(r < 2)
    def _():
        load_row().start()

    load_mine = pltpu.make_async_copy(a, mine, local_sem.at[2])
    load_mine.start()

    def arrived(b):
        own = (r == b // 2) & (c == b % 2)

        @pl.when(own)
        def _():
            own_copy(b).wait()

        @pl.when(jnp.logical_not(own))
        def _():
            send(pieces.at[b, c], pieces.at[b, c], s1_send.at[0], p_recv.at[b], (r, c)).wait_recv()

    def to_rows(b):
        for i in range(1, N_ROW):
            dst = lax.rem(r + i, N_ROW)
            yield send(pieces.at[b, c], pieces.at[b, c], s2_send.at[b % 2, i - 1], p_recv.at[b], (dst, c))

    def spread_rows(blocks):
        for b in blocks:
            @pl.when(r == b // 2)
            def _(b=b):
                arrived(b)
                for copy in to_rows(b):
                    copy.start()

    def to_cols(kind, dst):
        block = pieces.at[pl.ds(kind, 1 + 2 * kind), c]
        return send(block, block, s3_send.at[kind], s3_recv.at[kind], (r, dst))

    def spread_cols(kind, blocks):
        for b in blocks:
            @pl.when(r != b // 2)
            def _(b=b):
                arrived(b)

        @pl.loop(1, N_COL)
        def _(i):
            to_cols(kind, lax.rem(c + i, N_COL)).start()

    def all_pieces(kind):
        block = pieces.at[pl.ds(kind, 1 + 2 * kind), pl.ds(0, N_COL - 1)]
        return send(block, block, s3_send.at[kind], s3_recv.at[kind], (r, c))

    def forwards(b, half):
        z_one = (dist_y[b] == 0) & ((z == 0) | (z == 2) | (z == 3) | (z == 6))
        z_two = (dist_y[b] == 0) & ((z == 0) | (z == 2) | (z == 6))
        z_one_dst = jnp.where(z == 0, 2, jnp.where(z == 6, 5, lax.rem(z + 1, N_Z))) * N_Y + y
        z_two_dst = jnp.where(z == 0, 6, jnp.where(z == 2, 1, 7)) * N_Y + y
        if half == 0:
            y_on, y_dst = dist_y[b] <= 2, lax.rem(y + 1, N_Y)
        else:
            y_on, y_dst = dist_y[b] != 1, lax.rem(y + N_Y - 1, N_Y)
        return ((z_one, z_one_dst), (z_two, z_two_dst), (y_on, z * N_Y + y_dst))

    def chunk_copy(b, half, sub, i, way, dst, first=False):
        k = 2 * half + sub
        block = col.at[b, i, k]
        return send(a.at[i, 0, k] if first else block, block, col_send.at[b, k, i, way], col_recv.at[b, k, i], (r, dst))

    def relay(slot):
        for b in range(2):
            for half in range(2):
                dist = dist_z + (dist_y[b] if half == 0 else lax.rem(N_Y - dist_y[b], N_Y))
                m = slot - HOP * dist
                i = lax.div(m, 5)
                rest = lax.rem(m, 5) - half
                sub = lax.div(rest, 2)

                @pl.when((m >= 0) & ((rest == 0) | (rest == 2)) & (i < BR))
                def _(b=b, half=half, i=i, sub=sub):
                    @pl.when(jnp.logical_not(source[b]))
                    def _():
                        chunk_copy(b, half, sub, i, 0, c).wait_recv()
                        forward(b, half, sub, i)

                    @pl.when(source[b])
                    def _():
                        forward(b, half, sub, i, True)

    def forward(b, half, sub, i, first=False):
        for way, (on, dst) in enumerate(forwards(b, half)):
            @pl.when(on)
            def _(way=way, dst=dst):
                chunk_copy(b, half, sub, i, way, dst, first).start()

    def row_copy(i, dst):
        block = row.at[core]
        return send(block, block, row_send.at[i], row_recv.at[core], (dst, c))

    def row_out_start():
        @pl.when(r < 2)
        def _():
            for i in range(1, 4):
                row_copy(i, r + 2 * i).start()

    def row_swap():
        @pl.when(r >= 2)
        def _():
            row_copy(0, r).wait_recv()

        row_copy(0, r + 1 - 2 * core).start()

    spread_rows((0,))

    @pl.loop(0, PRE1)
    def _(slot):
        relay(slot)

    spread_cols(0, (0,))

    @pl.loop(PRE1, PRE2)
    def _(slot):
        relay(slot)

    @pl.when(r < 2)
    def _():
        load_row().wait()

    all_pieces(0).wait_recv()

    def whole(b):
        x = pieces[b].astype(F32).reshape(16, 2, 16, 128)
        return jnp.concatenate([x[:, 0].reshape(NB, 128), x[:, 1].reshape(NB, 128)], 1)

    load(whole(0), a1, a2)

    @pl.loop(0, 2)
    def _(step):
        @pl.when(step == 1)
        def _():
            all_pieces(1).wait_recv()
            l10[...] = nn(whole(2).astype(BF), uinv[0]).astype(BF)
            u01[...] = nn(linv[0], whole(1).astype(BF)).astype(BF)
            load((whole(3) - nn(l10[...], u01[...])).astype(BF).astype(F32), a1, a2)

        def tick(k):
            relay(PRE2 + step * 32 + k)
            if k == 1:
                @pl.when(step == 0)
                def _():
                    spread_rows((1, 2, 3))

            if k == 3:
                @pl.when(step == 0)
                def _():
                    spread_cols(1, (1, 2, 3))

            if k == 5:
                @pl.when(step == 0)
                def _():
                    row_out_start()

            if k == 13:
                @pl.when(step == 1)
                def _():
                    row_swap()

        factor(a1, a2, tick)
        pk, li, ui = results(a1, a2)
        packed[step] = pk.astype(BF)
        linv[step] = li.astype(BF)
        uinv[step] = ui.astype(BF)

    for b in range(2):
        @pl.when(source[b])
        def _(b=b):
            load_panel(b).wait()

    load_mine.wait()
    other = row.at[1 - core]
    send(other, other, row_send.at[0], row_recv.at[1 - core], (r, c)).wait_recv()
    for j in range(BC):
        h = j * N_COL + c
        u0 = jnp.where(h > 0, nn(linv[0], row[0, j].reshape(NB, NB)), 0.0).astype(BF)
        row1 = (row[1, j].reshape(NB, NB).astype(F32) - nn(l10[...], u0)).astype(BF)
        u[0, j] = u0
        u[1, j] = jnp.where(h > 1, nn(linv[1], row1), 0.0).astype(BF)

    @pl.loop(0, BR)
    def _(i):
        for k in range(TAIL):
            relay(PRE2 + 64 + TAIL * i + k)
        update(i, r, c, mine, col, packed, uinv, u01, u)

    for b in range(4):
        @pl.when((r == b // 2) & (c == b % 2))
        def _(b=b):
            block = pieces.at[0, pl.ds(0, N_COL - 1)]
            send(block, block, s1_send.at[0], p_recv.at[b], (r, c)).wait_send()

        @pl.when(r == b // 2)
        def _(b=b):
            for copy in to_rows(b):
                copy.wait_send()

    for kind in range(2):
        all_pieces(kind).wait_send()

    @pl.when(r < 2)
    def _():
        for i in range(1, 4):
            row_copy(i, r).wait_send()

    row_copy(0, r).wait_send()

    for b in range(2):
        for half in range(2):
            for way, (on, dst) in enumerate(forwards(b, half)):
                @pl.when(on)
                def _(b=b, half=half, way=way, dst=dst):
                    @pl.loop(0, BR)
                    def _(i):
                        for sub in range(2):
                            chunk_copy(b, half, sub, i, way, dst).wait_send()


def update(i, r, c, mine, col, packed, uinv, u01, u):
    g = i * N_ROW + r
    l0 = jnp.where(g > 0, nn(col[0, i].reshape(NB, NB), uinv[0]), 0.0).astype(BF)
    c1 = (col[1, i].reshape(NB, NB).astype(F32) - nn(l0, u01[...])).astype(BF)
    l1 = jnp.where(g > 1, nn(c1, uinv[1]), 0.0).astype(BF)

    def put(j, x):
        mine[i, j] = x.reshape(4, 64, NB)

    for j in range(BC):
        x = (mine[i, j].reshape(NB, NB).astype(F32) - nn(l0, u[0, j])).astype(BF)
        put(j, (x.astype(F32) - nn(l1, u[1, j])).astype(BF))

    @pl.when(c == 0)
    def _():
        put(0, jnp.where(g > 0, l0, packed[0]))

    @pl.when((c == 1) & (g > 0))
    def _():
        put(0, jnp.where(g > 1, l1, packed[1]))

    for k in range(2):
        @pl.when(g == k)
        def _(k=k):
            for j in range(BC):
                @pl.when(j * N_COL + c > k)
                def _(j=j):
                    put(j, u[k, j])


def on_device(matrix):
    dma = pltpu.SemaphoreType.DMA
    hbm = pl.BlockSpec(memory_space=pl.ANY)
    out = pl.pallas_call(
        gather_factor,
        out_shape=pltpu.VMEM((BR, BC, 4, 64, NB), BF),
        in_specs=[hbm],
        out_specs=pl.BlockSpec(memory_space=pltpu.VMEM),
        scratch_shapes=[
            pltpu.VMEM((2, NB, NB), BF),
            pltpu.VMEM((2, NB, NB), BF),
            pltpu.VMEM((2, NB, NB), BF),
            pltpu.VMEM((NB, NB), BF),
            pltpu.VMEM((NB, NB), BF),
            pltpu.VMEM((2, BC, NB, NB), BF),
            pltpu.VMEM((2, BR, 4, 64, NB), BF),
            pltpu.VMEM((2, BC, 4, 64, NB), BF),
            pltpu.VMEM((4, N_COL, 16, 128), BF),
            pltpu.VMEM((NB, 2 * NB), F32),
            pltpu.VMEM((NB, 2 * NB), F32),
            dma((1,)), dma((2, N_ROW - 1)), dma((2,)), dma((4,)), dma((2,)),
            dma((2, 4, BR, 3)), dma((2, 4, BR)), dma((4,)), dma((2,)), dma((3,)),
        ],
        compiler_params=pltpu.CompilerParams(
            collective_id=0, has_side_effects=True, vmem_limit_bytes=58 << 20
        ),
        name="gather_factor",
    )(matrix.transpose(0, 2, 1, 3).reshape(BR, BC, 4, 64, NB))
    return out.reshape(BR, BC, NB, NB).transpose(0, 2, 1, 3)


def solution(mesh):
    placed = (P(None, "row", None, "col"),)
    return jax.shard_map(
        on_device,
        mesh=mesh,
        in_specs=placed,
        out_specs=P(None, "row", None, "col"),
        check_vma=False,
    )
```

```python
import functools

import jax
import jax.experimental.pallas as pl
import jax.experimental.pallas.tpu as pltpu
import jax.numpy as jnp
from jax import lax
from jax.sharding import PartitionSpec as P

NB = 256
B = 64
BR, BC = 12, 3
N_ROW, N_COL, N_Y, N_Z = 8, 32, 4, 8
F32, BF = jnp.float32, jnp.bfloat16
MESH = pl.DeviceIdType.MESH
UNITS = 8
HOP = 2
LATE = 3
PRE1, PRE2 = 2, 6
GROUP = 3
TAIL = 1
assert all(PRE2 + 2 * UNITS + TAIL * (i + 1) >= 6 * HOP + GROUP * (i + 1) for i in range(BR // GROUP))


def recip(p):
    r = pl.reciprocal(p, approx=True)
    return r * (2.0 - p * r)

def bcast_lane(t, n):
    return jnp.broadcast_to(t[:, n:n + 1], (8, 128))

def bcast_row(t, j):
    return jnp.broadcast_to(t[j:j + 1, :], (8, 128))

def base(m1, m2, tick):
    sub = lax.broadcasted_iota(jnp.int32, (8, 128), 0)
    for k in range(8):
        tick(k)
        n = range(k, 8)
        v = {i: [bcast_lane(m1[i], 8 * k + j) for j in range(8)] for i in n}
        w = {i: [bcast_lane(m2[i], 8 * k + j) for j in range(8)] for i in n}
        scale = jnp.ones((8, 128), F32)
        for j in range(8):
            r = recip(bcast_row(v[k][j], j))
            scale = jnp.where(sub == j, r, scale)
            lv = {i: v[i][j] * r for i in n}
            lw = {i: w[i][j] * r for i in n}
            lv[k] = jnp.where(sub > j, lv[k], 0.0)
            lw[k] = jnp.where(sub > j, lw[k], 0.0)
            for t in range(j + 1, 8):
                a, b = bcast_row(v[k][t], j), bcast_row(w[k][t], j)
                for i in n:
                    v[i][t] = v[i][t] - lv[i] * a
                    w[i][t] = w[i][t] - lw[i] * b
            a, b = bcast_row(m1[k], j), bcast_row(m2[k], j)
            for i in n:
                m1[i] = m1[i] - lv[i] * a
                m2[i] = m2[i] - lw[i] * b
        m2[k] = m2[k] * scale
    return jnp.concatenate(m1, 0), jnp.concatenate(m2, 0)

def split(a):
    h = a.astype(BF)
    return h, (a - h.astype(F32)).astype(BF)

def dot3(a, b, nt=False):
    d = functools.partial(lax.dot_general, dimension_numbers=(((1,), (1 if nt else 0,)), ((), ())), preferred_element_type=F32)
    return d(a[0], b[0]) + (d(a[0], b[1]) + d(a[1], b[0]))

def factor(a1, a2, tick):
    eye = (lax.broadcasted_iota(jnp.int32, (B, B), 0) == lax.broadcasted_iota(jnp.int32, (B, B), 1)).astype(F32)
    for q in range(NB // B):
        s, e = q * B, (q + 1) * B
        d1 = jnp.concatenate([a1[s:e, s:e], eye], axis=1)
        d2 = jnp.concatenate([a2[s:e, s:e], eye], axis=1)
        m1, m2 = base(
            [d1[8 * i : 8 * i + 8] for i in range(8)], [d2[8 * i : 8 * i + 8] for i in range(8)],
            lambda k, q=q: tick(8 * q + k),
        )
        li, ui = split(m1[:, B:]), split(m2[:, B:])
        p1, p2 = dot3(li, split(a1[s:e, :])), dot3(ui, split(a2[s:e, :]))
        if e < NB:
            l21 = split(dot3(split(a1[e:, s:e]), ui, True))
            u12 = split(dot3(split(a2[e:, s:e]), li, True))
            a1[e:, :] = a1[e:, :] - dot3(l21, split(p1))
            a2[e:, :] = a2[e:, :] - dot3(u12, split(p2))
        a1[s:e, :] = p1
        a2[s:e, :] = p2
        a1[s:e, s:e] = m1[:, :B]
        a2[s:e, s:e] = m2[:, :B]


def load(a, a1, a2):
    ri = lax.broadcasted_iota(jnp.int32, (NB, NB), 0)
    ci = lax.broadcasted_iota(jnp.int32, (NB, NB), 1)
    eye = (ri == ci).astype(F32)
    for ref, x in ((a1, a), (a2, jnp.transpose(a))):
        ref[:, :NB] = x
        ref[:, NB:] = eye


def results(a1, a2):
    ri = lax.broadcasted_iota(jnp.int32, (NB, NB), 0)
    ci = lax.broadcasted_iota(jnp.int32, (NB, NB), 1)
    packed = jnp.where(ri <= ci, a1[:, :NB], jnp.transpose(a2[:, :NB]))
    return packed, a1[:, NB:], jnp.transpose(a2[:, NB:])


def nn(a, b):
    return jnp.dot(a, b, preferred_element_type=F32)


def gather_factor(
    a, mine, packed, linv, uinv, l10, u01, u, col, row, pieces, a1, a2,
    s1_send, s2_send, s3_send, p_recv, s3_recv,
    col_send, col_recv, row_send, row_recv, local_sem,
):
    r, c = lax.axis_index("row"), lax.axis_index("col")
    z, y = lax.div(c, N_Y), lax.rem(c, N_Y)
    core = lax.rem(r, 2)

    def send(src, dst, ssem, rsem, dev):
        return pltpu.make_async_remote_copy(
            src_ref=src, dst_ref=dst, send_sem=ssem, recv_sem=rsem, device_id=dev, device_id_type=MESH
        )

    barrier = pltpu.get_barrier_semaphore()

    @pl.loop(1, N_COL)
    def _(i):
        pl.semaphore_signal(barrier, inc=1, device_id=(r, lax.rem(c + i, N_COL)), device_id_type=MESH)

    @pl.loop(1, N_ROW)
    def _(i):
        pl.semaphore_signal(barrier, inc=1, device_id=(lax.rem(r + i, N_ROW), c), device_id_type=MESH)

    pl.semaphore_wait(barrier, N_COL - 1 + N_ROW - 1)

    def diag_piece(p):
        return a.at[0, 0, lax.div(p, 16), pl.ds(pl.multiple_of(lax.rem(lax.div(p, 2), 8) * 16, 16), 16),
                    pl.ds(pl.multiple_of(lax.rem(p, 2) * 128, 128), 128)]

    def own_copy(b):
        return pltpu.make_async_copy(diag_piece(c), pieces.at[b, c], p_recv.at[b])

    for b in range(4):
        @pl.when((r == b // 2) & (c == b % 2))
        def _(b=b):
            @pl.loop(1, N_COL)
            def _(i):
                dst = lax.rem(c + i, N_COL)
                send(diag_piece(dst), pieces.at[b, dst], s1_send.at[0], p_recv.at[b], (r, dst)).start()

            own_copy(b).start()

    dist_z = jnp.where(z == 0, 0, jnp.where(lax.rem(z, 4) == 2, 1, jnp.where(z == 4, 3, 2)))
    dist_y = [lax.rem(y - b + N_Y, N_Y) for b in range(2)]
    source = [(z == 0) & (dist_y[b] == 0) for b in range(2)]

    def load_panel(b):
        return pltpu.make_async_copy(a.at[:, 0], col.at[b], local_sem.at[0])

    def load_row():
        return pltpu.make_async_copy(a.at[0], row.at[core], local_sem.at[1])

    for b in range(2):
        @pl.when(source[b])
        def _(b=b):
            load_panel(b).start()

    @pl.when(r < 2)
    def _():
        load_row().start()

    load_mine = pltpu.make_async_copy(a, mine, local_sem.at[2])
    load_mine.start()

    def arrived(b):
        own = (r == b // 2) & (c == b % 2)

        @pl.when(own)
        def _():
            own_copy(b).wait()

        @pl.when(jnp.logical_not(own))
        def _():
            send(pieces.at[b, c], pieces.at[b, c], s1_send.at[0], p_recv.at[b], (r, c)).wait_recv()

    def to_rows(b):
        for i in range(1, N_ROW):
            dst = lax.rem(r + i, N_ROW)
            yield send(pieces.at[b, c], pieces.at[b, c], s2_send.at[b % 2, i - 1], p_recv.at[b], (dst, c))

    def spread_rows(blocks):
        for b in blocks:
            @pl.when(r == b // 2)
            def _(b=b):
                arrived(b)
                for copy in to_rows(b):
                    copy.start()

    def to_cols(kind, dst):
        block = pieces.at[pl.ds(kind, 1 + 2 * kind), c]
        return send(block, block, s3_send.at[kind], s3_recv.at[kind], (r, dst))

    def spread_cols(kind, blocks):
        for b in blocks:
            @pl.when(r != b // 2)
            def _(b=b):
                arrived(b)

        @pl.loop(1, N_COL)
        def _(i):
            to_cols(kind, lax.rem(c + i, N_COL)).start()

    def all_pieces(kind):
        block = pieces.at[pl.ds(kind, 1 + 2 * kind), pl.ds(0, N_COL - 1)]
        return send(block, block, s3_send.at[kind], s3_recv.at[kind], (r, c))

    lanes = [[0, 3], [1, 2]]

    def from_lane(b, half):
        return lax.rem(y - lanes[b][half] + N_Y, N_Y)

    def ring(d):
        return jnp.minimum(d, N_Y - d)

    def distance(b, half):
        first = ring(dist_y[b]) + (LATE * jnp.minimum(dist_y[b], 1) if half == 0 else 0)
        return jnp.where(z == 0, first, dist_z + half + ring(from_lane(b, half)))

    def along_z(b, half, i):
        on = from_lane(b, half) == 0
        z_one = on & ((z == 0) | (z == 2) | (z == 3) | (z == 6))
        z_two = on & ((z == 0) | (z == 2) | (z == 6))
        z_one_dst = jnp.where(z == 0, 2, jnp.where(z == 6, 5, lax.rem(z + 1, N_Z))) * N_Y + y
        z_two_dst = jnp.where(z == 0, 6, jnp.where(z == 2, 1, 7)) * N_Y + y
        return ((0, z_one, z_one_dst), (1, z_two, z_two_dst))

    def along_y(b, half, i):
        d, e, odd = from_lane(b, half), dist_y[b], lax.rem(i, 2)
        here = (z == 0) & ((e == 0) | (e == (3, 1)[b]))
        up = (e == 0) if b == 0 else here
        down = here if b == 0 else (e == 0)
        up = ((z == 0) & up) | ((z > 0) & ((d == 0) | ((d == 1) & (odd == 0))))
        down = ((z == 0) & down) | ((z > 0) & ((d == 0) | ((d == 3) & (odd == 1))))
        return ((2, up, z * N_Y + lax.rem(y + 1, N_Y)), (3, down, z * N_Y + lax.rem(y + N_Y - 1, N_Y)))

    def chunk_copy(b, half, i, way, dst, first=False):
        block = col.at[b, i, half]
        return send(a.at[i, 0, half] if first else block, block, col_send.at[b, half, i, way],
                    col_recv.at[b, half, i], (r, dst))

    def relay(unit, half):
        for b in range(2):
            i = unit - HOP * distance(b, half)

            @pl.when(jnp.logical_not(source[b]) & (i >= 0) & (i < BR))
            def _(b=b, i=i):
                chunk_copy(b, half, i, 0, c).wait_recv()
                forward(b, half, i, (along_z, along_y))

            @pl.when(source[b])
            def _(b=b):
                for ways, late in ((along_z, 0), (along_y, HOP * LATE if half == 0 else 0)):
                    i = unit - late

                    @pl.when((i >= 0) & (i < BR))
                    def _(ways=ways, i=i):
                        forward(b, half, i, (ways,), True)

    def forward(b, half, i, kinds, first=False):
        for kind in kinds:
            for way, on, dst in kind(b, half, i):
                @pl.when(on)
                def _(way=way, dst=dst):
                    chunk_copy(b, half, i, way, dst, first).start()

    def row_copy(i, dst):
        block = row.at[core]
        return send(block, block, row_send.at[i], row_recv.at[core], (dst, c))

    def row_out_start():
        @pl.when(r < 2)
        def _():
            for i in range(1, 4):
                row_copy(i, r + 2 * i).start()

    def row_swap():
        @pl.when(r >= 2)
        def _():
            row_copy(0, r).wait_recv()

        row_copy(0, r + 1 - 2 * core).start()

    @pl.loop(0, PRE1)
    def _(unit):
        relay(unit, 1)
        relay(unit, 0)

    spread_rows((0,))

    spread_cols(0, (0,))

    @pl.loop(PRE1, PRE2)
    def _(unit):
        relay(unit, 1)
        relay(unit, 0)

    @pl.when(r < 2)
    def _():
        load_row().wait()

    all_pieces(0).wait_recv()

    def whole(b):
        x = pieces[b].astype(F32).reshape(16, 2, 16, 128)
        return jnp.concatenate([x[:, 0].reshape(NB, 128), x[:, 1].reshape(NB, 128)], 1)

    load(whole(0), a1, a2)

    halves = [[(32 * i + 16 * (1 - half)) // UNITS for i in range(UNITS)] for half in range(2)]

    @pl.loop(0, 2)
    def _(step):
        @pl.when(step == 1)
        def _():
            all_pieces(1).wait_recv()
            l10[...] = nn(whole(2).astype(BF), uinv[0]).astype(BF)
            u01[...] = nn(linv[0], whole(1).astype(BF)).astype(BF)
            load((whole(3) - nn(l10[...], u01[...])).astype(BF).astype(F32), a1, a2)

        def tick(k):
            for half in (1, 0):
                if k in halves[half]:
                    relay(PRE2 + step * UNITS + halves[half].index(k), half)

            if k == 1:
                @pl.when(step == 0)
                def _():
                    spread_rows((1, 2, 3))

            if k == 3:
                @pl.when(step == 0)
                def _():
                    spread_cols(1, (1, 2, 3))

            if k == 5:
                @pl.when(step == 0)
                def _():
                    row_out_start()

            if k == 13:
                @pl.when(step == 1)
                def _():
                    row_swap()

        factor(a1, a2, tick)
        pk, li, ui = results(a1, a2)
        packed[step] = pk.astype(BF)
        linv[step] = li.astype(BF)
        uinv[step] = ui.astype(BF)

    for b in range(2):
        @pl.when(source[b])
        def _(b=b):
            load_panel(b).wait()

    load_mine.wait()
    other = row.at[1 - core]
    send(other, other, row_send.at[0], row_recv.at[1 - core], (r, c)).wait_recv()
    for j in range(BC):
        h = j * N_COL + c
        u0 = jnp.where(h > 0, nn(linv[0], row[0, j].reshape(NB, NB)), 0.0).astype(BF)
        row1 = (row[1, j].reshape(NB, NB).astype(F32) - nn(l10[...], u0)).astype(BF)
        u[0, j] = u0
        u[1, j] = jnp.where(h > 1, nn(linv[1], row1), 0.0).astype(BF)

    @pl.loop(0, BR // GROUP)
    def _(i):
        for k in range(TAIL):
            for half in (1, 0):
                relay(PRE2 + 2 * UNITS + TAIL * i + k, half)

        update(i, r, c, mine, col, packed, uinv, u01, u)

    for b in range(4):
        @pl.when((r == b // 2) & (c == b % 2))
        def _(b=b):
            block = pieces.at[0, pl.ds(0, N_COL - 1)]
            send(block, block, s1_send.at[0], p_recv.at[b], (r, c)).wait_send()

        @pl.when(r == b // 2)
        def _(b=b):
            for copy in to_rows(b):
                copy.wait_send()

    for kind in range(2):
        all_pieces(kind).wait_send()

    @pl.when(r < 2)
    def _():
        for i in range(1, 4):
            row_copy(i, r).wait_send()

    row_copy(0, r).wait_send()

    for b in range(2):
        for half in range(2):
            @pl.loop(0, BR)
            def _(i, b=b, half=half):
                for way, on, dst in along_z(b, half, i) + along_y(b, half, i):
                    @pl.when(on)
                    def _(way=way, dst=dst):
                        chunk_copy(b, half, i, way, dst).wait_send()


def update(i, r, c, mine, col, packed, uinv, u01, u):
    rows = pl.ds(pl.multiple_of(i * GROUP, GROUP), GROUP)
    high = GROUP * NB
    later = (lax.broadcasted_iota(jnp.int32, (high, NB), 0) >= NB) | (i > 0)
    l0 = jnp.where(later | (r > 0), nn(col[0, rows].reshape(high, NB), uinv[0]), 0.0).astype(BF)
    c1 = (col[1, rows].reshape(high, NB).astype(F32) - nn(l0, u01[...])).astype(BF)
    l1 = jnp.where(later | (r > 1), nn(c1, uinv[1]), 0.0).astype(BF)
    for j in range(BC):
        x = (mine[rows, j].reshape(high, NB).astype(F32) - nn(l0, u[0, j])).astype(BF)
        x = (x.astype(F32) - nn(l1, u[1, j])).astype(BF)
        mine[rows, j] = x.reshape(GROUP, 2, 128, NB)

    @pl.when(c == 0)
    def _():
        mine[rows, 0] = l0.reshape(GROUP, 2, 128, NB)

    @pl.when(c == 1)
    def _():
        kept = mine[rows, 0].reshape(high, NB)
        mine[rows, 0] = jnp.where(later | (r > 1), l1, kept).reshape(GROUP, 2, 128, NB)

    for k in range(2):
        @pl.when((i == 0) & (r == k))
        def _(k=k):
            for j in range(BC):
                @pl.when(j * N_COL + c > k)
                def _(j=j):
                    mine[0, j] = u[k, j].reshape(2, 128, NB)

            @pl.when(c == k)
            def _():
                mine[0, 0] = packed[k].reshape(2, 128, NB)


def on_device(matrix):
    dma = pltpu.SemaphoreType.DMA
    hbm = pl.BlockSpec(memory_space=pl.ANY)
    out = pl.pallas_call(
        gather_factor,
        out_shape=pltpu.VMEM((BR, BC, 2, 128, NB), BF),
        in_specs=[hbm],
        out_specs=pl.BlockSpec(memory_space=pltpu.VMEM),
        scratch_shapes=[
            pltpu.VMEM((2, NB, NB), BF),
            pltpu.VMEM((2, NB, NB), BF),
            pltpu.VMEM((2, NB, NB), BF),
            pltpu.VMEM((NB, NB), BF),
            pltpu.VMEM((NB, NB), BF),
            pltpu.VMEM((2, BC, NB, NB), BF),
            pltpu.VMEM((2, BR, 2, 128, NB), BF),
            pltpu.VMEM((2, BC, 2, 128, NB), BF),
            pltpu.VMEM((4, N_COL, 16, 128), BF),
            pltpu.VMEM((NB, 2 * NB), F32),
            pltpu.VMEM((NB, 2 * NB), F32),
            dma((1,)), dma((2, N_ROW - 1)), dma((2,)), dma((4,)), dma((2,)),
            dma((2, 2, BR, 4)), dma((2, 2, BR)), dma((4,)), dma((2,)), dma((3,)),
        ],
        compiler_params=pltpu.CompilerParams(
            collective_id=0, has_side_effects=True, vmem_limit_bytes=58 << 20
        ),
        name="gather_factor",
    )(matrix.transpose(0, 2, 1, 3).reshape(BR, BC, 2, 128, NB))
    return out.reshape(BR, BC, NB, NB).transpose(0, 2, 1, 3)


def solution(mesh):
    placed = (P(None, "row", None, "col"),)
    return jax.shard_map(
        on_device,
        mesh=mesh,
        in_specs=placed,
        out_specs=P(None, "row", None, "col"),
        check_vma=False,
    )
```

```python
import functools

import jax
import jax.experimental.pallas as pl
import jax.experimental.pallas.tpu as pltpu
import jax.numpy as jnp
from jax import lax
from jax.sharding import PartitionSpec as P

NB = 256
B = 64
BR, BC = 12, 3
N_ROW, N_COL, N_Y, N_Z = 8, 32, 4, 8
F32, BF = jnp.float32, jnp.bfloat16
MESH = pl.DeviceIdType.MESH
UNITS = 7
HOP = 2
LATE = 3
PRE1, PRE2 = 3, 8
GROUP = 3
TAIL = 1
assert all(PRE2 + 2 * UNITS + TAIL * (i + 1) >= 6 * HOP + GROUP * (i + 1) for i in range(BR // GROUP))


def recip(p):
    r = pl.reciprocal(p, approx=True)
    return r * (2.0 - p * r)

def bcast_lane(t, n):
    return jnp.broadcast_to(t[:, n:n + 1], (8, 128))

def bcast_row(t, j):
    return jnp.broadcast_to(t[j:j + 1, :], (8, 128))

def base(m1, m2, tick):
    sub = lax.broadcasted_iota(jnp.int32, (8, 128), 0)
    for k in range(8):
        tick(k)
        n = range(k, 8)
        v = {i: [bcast_lane(m1[i], 8 * k + j) for j in range(8)] for i in n}
        w = {i: [bcast_lane(m2[i], 8 * k + j) for j in range(8)] for i in n}
        scale = jnp.ones((8, 128), F32)
        for j in range(8):
            r = recip(bcast_row(v[k][j], j))
            scale = jnp.where(sub == j, r, scale)
            lv = {i: v[i][j] * r for i in n}
            lw = {i: w[i][j] * r for i in n}
            lv[k] = jnp.where(sub > j, lv[k], 0.0)
            lw[k] = jnp.where(sub > j, lw[k], 0.0)
            for t in range(j + 1, 8):
                a, b = bcast_row(v[k][t], j), bcast_row(w[k][t], j)
                for i in n:
                    v[i][t] = v[i][t] - lv[i] * a
                    w[i][t] = w[i][t] - lw[i] * b
            a, b = bcast_row(m1[k], j), bcast_row(m2[k], j)
            for i in n:
                m1[i] = m1[i] - lv[i] * a
                m2[i] = m2[i] - lw[i] * b
        m2[k] = m2[k] * scale
    return jnp.concatenate(m1, 0), jnp.concatenate(m2, 0)

def split(a):
    h = a.astype(BF)
    return h, (a - h.astype(F32)).astype(BF)

def dot3(a, b, nt=False):
    d = functools.partial(lax.dot_general, dimension_numbers=(((1,), (1 if nt else 0,)), ((), ())), preferred_element_type=F32)
    return d(a[0], b[0]) + (d(a[0], b[1]) + d(a[1], b[0]))

def factor(a1, a2, tick):
    eye = (lax.broadcasted_iota(jnp.int32, (B, B), 0) == lax.broadcasted_iota(jnp.int32, (B, B), 1)).astype(F32)
    for q in range(NB // B):
        s, e = q * B, (q + 1) * B
        d1 = jnp.concatenate([a1[s:e, s:e], eye], axis=1)
        d2 = jnp.concatenate([a2[s:e, s:e], eye], axis=1)
        m1, m2 = base(
            [d1[8 * i : 8 * i + 8] for i in range(8)], [d2[8 * i : 8 * i + 8] for i in range(8)],
            lambda k, q=q: tick(8 * q + k),
        )
        li, ui = split(m1[:, B:]), split(m2[:, B:])
        p1, p2 = dot3(li, split(a1[s:e, :])), dot3(ui, split(a2[s:e, :]))
        if e < NB:
            l21 = split(dot3(split(a1[e:, s:e]), ui, True))
            u12 = split(dot3(split(a2[e:, s:e]), li, True))
            a1[e:, :] = a1[e:, :] - dot3(l21, split(p1))
            a2[e:, :] = a2[e:, :] - dot3(u12, split(p2))
        a1[s:e, :] = p1
        a2[s:e, :] = p2
        a1[s:e, s:e] = m1[:, :B]
        a2[s:e, s:e] = m2[:, :B]


def load(a, a1, a2):
    ri = lax.broadcasted_iota(jnp.int32, (NB, NB), 0)
    ci = lax.broadcasted_iota(jnp.int32, (NB, NB), 1)
    eye = (ri == ci).astype(F32)
    for ref, x in ((a1, a), (a2, jnp.transpose(a))):
        ref[:, :NB] = x
        ref[:, NB:] = eye


def results(a1, a2):
    ri = lax.broadcasted_iota(jnp.int32, (NB, NB), 0)
    ci = lax.broadcasted_iota(jnp.int32, (NB, NB), 1)
    packed = jnp.where(ri <= ci, a1[:, :NB], jnp.transpose(a2[:, :NB]))
    return packed, a1[:, NB:], jnp.transpose(a2[:, NB:])


def nn(a, b):
    return jnp.dot(a, b, preferred_element_type=F32)


def gather_factor(
    a, mine, packed, linv, uinv, l10, u01, u, col, row, pieces, a1, a2,
    s1_send, s2_send, s3_send, p_recv, s3_recv,
    col_send, col_recv, row_send, row_recv, local_sem,
):
    r, c = lax.axis_index("row"), lax.axis_index("col")
    z, y = lax.div(c, N_Y), lax.rem(c, N_Y)
    core = lax.rem(r, 2)

    def send(src, dst, ssem, rsem, dev):
        return pltpu.make_async_remote_copy(
            src_ref=src, dst_ref=dst, send_sem=ssem, recv_sem=rsem, device_id=dev, device_id_type=MESH
        )

    barrier = pltpu.get_barrier_semaphore()

    @pl.loop(1, N_COL)
    def _(i):
        pl.semaphore_signal(barrier, inc=1, device_id=(r, lax.rem(c + i, N_COL)), device_id_type=MESH)

    @pl.loop(1, N_ROW)
    def _(i):
        pl.semaphore_signal(barrier, inc=1, device_id=(lax.rem(r + i, N_ROW), c), device_id_type=MESH)

    pl.semaphore_wait(barrier, N_COL - 1 + N_ROW - 1)

    def diag_piece(p):
        return a.at[0, 0, lax.div(p, 16), pl.ds(pl.multiple_of(lax.rem(lax.div(p, 2), 8) * 16, 16), 16),
                    pl.ds(pl.multiple_of(lax.rem(p, 2) * 128, 128), 128)]

    def own_copy(b):
        return pltpu.make_async_copy(diag_piece(c), pieces.at[b, c], p_recv.at[b])

    for b in range(4):
        @pl.when((r == b // 2) & (c == b % 2))
        def _(b=b):
            @pl.loop(1, N_COL)
            def _(i):
                dst = lax.rem(c + i, N_COL)
                send(diag_piece(dst), pieces.at[b, dst], s1_send.at[0], p_recv.at[b], (r, dst)).start()

            own_copy(b).start()

    dist_z = jnp.where(z == 0, 0, jnp.where(lax.rem(z, 4) == 2, 1, jnp.where(z == 4, 3, 2)))
    dist_y = [lax.rem(y - b + N_Y, N_Y) for b in range(2)]
    source = [(z == 0) & (dist_y[b] == 0) for b in range(2)]

    def load_panel(b):
        return pltpu.make_async_copy(a.at[:, 0], col.at[b], local_sem.at[0])

    def load_row():
        return pltpu.make_async_copy(a.at[0], row.at[core], local_sem.at[1])

    for b in range(2):
        @pl.when(source[b])
        def _(b=b):
            load_panel(b).start()

    @pl.when(r < 2)
    def _():
        load_row().start()

    load_mine = pltpu.make_async_copy(a, mine, local_sem.at[2])
    load_mine.start()

    def arrived(b):
        own = (r == b // 2) & (c == b % 2)

        @pl.when(own)
        def _():
            own_copy(b).wait()

        @pl.when(jnp.logical_not(own))
        def _():
            send(pieces.at[b, c], pieces.at[b, c], s1_send.at[0], p_recv.at[b], (r, c)).wait_recv()

    def to_rows(b):
        for i in range(1, N_ROW):
            dst = lax.rem(r + i, N_ROW)
            yield send(pieces.at[b, c], pieces.at[b, c], s2_send.at[b % 2, i - 1], p_recv.at[b], (dst, c))

    def spread_rows(blocks):
        for b in blocks:
            @pl.when(r == b // 2)
            def _(b=b):
                arrived(b)
                for copy in to_rows(b):
                    copy.start()

    def to_cols(kind, dst):
        block = pieces.at[pl.ds(kind, 1 + 2 * kind), c]
        return send(block, block, s3_send.at[kind], s3_recv.at[kind], (r, dst))

    def spread_cols(kind, blocks):
        for b in blocks:
            @pl.when(r != b // 2)
            def _(b=b):
                arrived(b)

        @pl.loop(1, N_COL)
        def _(i):
            to_cols(kind, lax.rem(c + i, N_COL)).start()

    def all_pieces(kind):
        block = pieces.at[pl.ds(kind, 1 + 2 * kind), pl.ds(0, N_COL - 1)]
        return send(block, block, s3_send.at[kind], s3_recv.at[kind], (r, c))

    lanes = [[0, 3], [1, 2]]

    def from_lane(b, half):
        return lax.rem(y - lanes[b][half] + N_Y, N_Y)

    def ring(d):
        return jnp.minimum(d, N_Y - d)

    def distance(b, half):
        first = ring(dist_y[b]) + (LATE * jnp.minimum(dist_y[b], 1) if half == 0 else 0)
        return jnp.where(z == 0, first, dist_z + half + ring(from_lane(b, half)))

    def along_z(b, half, i):
        on = from_lane(b, half) == 0
        z_one = on & ((z == 0) | (z == 2) | (z == 3) | (z == 6))
        z_two = on & ((z == 0) | (z == 2) | (z == 6))
        z_one_dst = jnp.where(z == 0, 2, jnp.where(z == 6, 5, lax.rem(z + 1, N_Z))) * N_Y + y
        z_two_dst = jnp.where(z == 0, 6, jnp.where(z == 2, 1, 7)) * N_Y + y
        return ((0, z_one, z_one_dst), (1, z_two, z_two_dst))

    def along_y(b, half, i):
        d, e, odd = from_lane(b, half), dist_y[b], lax.rem(i, 2)
        here = (z == 0) & ((e == 0) | (e == (3, 1)[b]))
        up = (e == 0) if b == 0 else here
        down = here if b == 0 else (e == 0)
        up = ((z == 0) & up) | ((z > 0) & ((d == 0) | ((d == 1) & (odd == 0))))
        down = ((z == 0) & down) | ((z > 0) & ((d == 0) | ((d == 3) & (odd == 1))))
        return ((2, up, z * N_Y + lax.rem(y + 1, N_Y)), (3, down, z * N_Y + lax.rem(y + N_Y - 1, N_Y)))

    def chunk_copy(b, half, i, way, dst, first=False):
        block = col.at[b, i, half]
        return send(a.at[i, 0, half] if first else block, block, col_send.at[b, half, i, way],
                    col_recv.at[b, half, i], (r, dst))

    def relay(unit, half):
        for b in range(2):
            i = unit - HOP * distance(b, half)

            @pl.when(jnp.logical_not(source[b]) & (i >= 0) & (i < BR))
            def _(b=b, i=i):
                chunk_copy(b, half, i, 0, c).wait_recv()
                forward(b, half, i, (along_z, along_y))

            @pl.when(source[b])
            def _(b=b):
                for ways, late in ((along_z, 0), (along_y, HOP * LATE if half == 0 else 0)):
                    i = unit - late

                    @pl.when((i >= 0) & (i < BR))
                    def _(ways=ways, i=i):
                        forward(b, half, i, (ways,), True)

    def forward(b, half, i, kinds, first=False):
        for kind in kinds:
            for way, on, dst in kind(b, half, i):
                @pl.when(on)
                def _(way=way, dst=dst):
                    chunk_copy(b, half, i, way, dst, first).start()

    def row_copy(i, dst):
        block = row.at[core]
        return send(block, block, row_send.at[i], row_recv.at[core], (dst, c))

    def row_out_start():
        @pl.when(r < 2)
        def _():
            for i in range(1, 4):
                row_copy(i, r + 2 * i).start()

    def row_swap():
        @pl.when(r >= 2)
        def _():
            row_copy(0, r).wait_recv()

        row_copy(0, r + 1 - 2 * core).start()

    @pl.loop(0, PRE1)
    def _(unit):
        relay(unit, 1)
        relay(unit, 0)

    spread_rows((0,))

    spread_cols(0, (0,))

    @pl.loop(PRE1, PRE2)
    def _(unit):
        relay(unit, 1)
        relay(unit, 0)

    @pl.when(r < 2)
    def _():
        load_row().wait()

    all_pieces(0).wait_recv()

    def whole(b):
        x = pieces[b].astype(F32).reshape(16, 2, 16, 128)
        return jnp.concatenate([x[:, 0].reshape(NB, 128), x[:, 1].reshape(NB, 128)], 1)

    load(whole(0), a1, a2)

    halves = [[(32 * i + 16 * (1 - half)) // UNITS for i in range(UNITS)] for half in range(2)]

    @pl.loop(0, 2)
    def _(step):
        @pl.when(step == 1)
        def _():
            all_pieces(1).wait_recv()
            l10[...] = nn(whole(2).astype(BF), uinv[0]).astype(BF)
            u01[...] = nn(linv[0], whole(1).astype(BF)).astype(BF)
            load((whole(3) - nn(l10[...], u01[...])).astype(BF).astype(F32), a1, a2)

        def tick(k):
            for half in (1, 0):
                if k in halves[half]:
                    relay(PRE2 + step * UNITS + halves[half].index(k), half)

            if k == 1:
                @pl.when(step == 0)
                def _():
                    spread_rows((1, 2, 3))

            if k == 3:
                @pl.when(step == 0)
                def _():
                    spread_cols(1, (1, 2, 3))

            if k == 5:
                @pl.when(step == 0)
                def _():
                    row_out_start()

            if k == 13:
                @pl.when(step == 1)
                def _():
                    row_swap()

        factor(a1, a2, tick)
        pk, li, ui = results(a1, a2)
        packed[step] = pk.astype(BF)
        linv[step] = li.astype(BF)
        uinv[step] = ui.astype(BF)

    for b in range(2):
        @pl.when(source[b])
        def _(b=b):
            load_panel(b).wait()

    load_mine.wait()
    other = row.at[1 - core]
    send(other, other, row_send.at[0], row_recv.at[1 - core], (r, c)).wait_recv()
    for j in range(BC):
        h = j * N_COL + c
        u0 = jnp.where(h > 0, nn(linv[0], row[0, j].reshape(NB, NB)), 0.0).astype(BF)
        row1 = (row[1, j].reshape(NB, NB).astype(F32) - nn(l10[...], u0)).astype(BF)
        u[0, j] = u0
        u[1, j] = jnp.where(h > 1, nn(linv[1], row1), 0.0).astype(BF)

    @pl.loop(0, BR // GROUP)
    def _(i):
        for k in range(TAIL):
            for half in (1, 0):
                relay(PRE2 + 2 * UNITS + TAIL * i + k, half)

        update(i, r, c, mine, col, packed, uinv, u01, u)

    for b in range(4):
        @pl.when((r == b // 2) & (c == b % 2))
        def _(b=b):
            block = pieces.at[0, pl.ds(0, N_COL - 1)]
            send(block, block, s1_send.at[0], p_recv.at[b], (r, c)).wait_send()

        @pl.when(r == b // 2)
        def _(b=b):
            for copy in to_rows(b):
                copy.wait_send()

    for kind in range(2):
        all_pieces(kind).wait_send()

    @pl.when(r < 2)
    def _():
        for i in range(1, 4):
            row_copy(i, r).wait_send()

    row_copy(0, r).wait_send()

    for b in range(2):
        for half in range(2):
            @pl.loop(0, BR)
            def _(i, b=b, half=half):
                for way, on, dst in along_z(b, half, i) + along_y(b, half, i):
                    @pl.when(on)
                    def _(way=way, dst=dst):
                        chunk_copy(b, half, i, way, dst).wait_send()


def update(i, r, c, mine, col, packed, uinv, u01, u):
    rows = pl.ds(pl.multiple_of(i * GROUP, GROUP), GROUP)
    high = GROUP * NB
    later = (lax.broadcasted_iota(jnp.int32, (high, NB), 0) >= NB) | (i > 0)
    l0 = jnp.where(later | (r > 0), nn(col[0, rows].reshape(high, NB), uinv[0]), 0.0).astype(BF)
    c1 = (col[1, rows].reshape(high, NB).astype(F32) - nn(l0, u01[...])).astype(BF)
    l1 = jnp.where(later | (r > 1), nn(c1, uinv[1]), 0.0).astype(BF)
    for j in range(BC):
        x = (mine[rows, j].reshape(high, NB).astype(F32) - nn(l0, u[0, j])).astype(BF)
        x = (x.astype(F32) - nn(l1, u[1, j])).astype(BF)
        mine[rows, j] = x.reshape(GROUP, 2, 128, NB)

    @pl.when(c == 0)
    def _():
        mine[rows, 0] = l0.reshape(GROUP, 2, 128, NB)

    @pl.when(c == 1)
    def _():
        kept = mine[rows, 0].reshape(high, NB)
        mine[rows, 0] = jnp.where(later | (r > 1), l1, kept).reshape(GROUP, 2, 128, NB)

    for k in range(2):
        @pl.when((i == 0) & (r == k))
        def _(k=k):
            for j in range(BC):
                @pl.when(j * N_COL + c > k)
                def _(j=j):
                    mine[0, j] = u[k, j].reshape(2, 128, NB)

            @pl.when(c == k)
            def _():
                mine[0, 0] = packed[k].reshape(2, 128, NB)


def on_device(matrix):
    dma = pltpu.SemaphoreType.DMA
    hbm = pl.BlockSpec(memory_space=pl.ANY)
    out = pl.pallas_call(
        gather_factor,
        out_shape=pltpu.VMEM((BR, BC, 2, 128, NB), BF),
        in_specs=[hbm],
        out_specs=pl.BlockSpec(memory_space=pltpu.VMEM),
        scratch_shapes=[
            pltpu.VMEM((2, NB, NB), BF),
            pltpu.VMEM((2, NB, NB), BF),
            pltpu.VMEM((2, NB, NB), BF),
            pltpu.VMEM((NB, NB), BF),
            pltpu.VMEM((NB, NB), BF),
            pltpu.VMEM((2, BC, NB, NB), BF),
            pltpu.VMEM((2, BR, 2, 128, NB), BF),
            pltpu.VMEM((2, BC, 2, 128, NB), BF),
            pltpu.VMEM((4, N_COL, 16, 128), BF),
            pltpu.VMEM((NB, 2 * NB), F32),
            pltpu.VMEM((NB, 2 * NB), F32),
            dma((1,)), dma((2, N_ROW - 1)), dma((2,)), dma((4,)), dma((2,)),
            dma((2, 2, BR, 4)), dma((2, 2, BR)), dma((4,)), dma((2,)), dma((3,)),
        ],
        compiler_params=pltpu.CompilerParams(
            collective_id=0, has_side_effects=True, vmem_limit_bytes=58 << 20
        ),
        name="gather_factor",
    )(matrix.transpose(0, 2, 1, 3).reshape(BR, BC, 2, 128, NB))
    return out.reshape(BR, BC, NB, NB).transpose(0, 2, 1, 3)


def solution(mesh):
    placed = (P(None, "row", None, "col"),)
    return jax.shard_map(
        on_device,
        mesh=mesh,
        in_specs=placed,
        out_specs=P(None, "row", None, "col"),
        check_vma=False,
    )
```
